32 devices in a mesh: section: 2 (over core), dev: 16 (over z, y, x).
Axes of the slice: x: 2, y: 2, z: 4, core: 2. Of those that a mesh axis runs over, the one named last changes fastest.
Arguments:
- token_ids: int32 [1, 16], replicated, may hold values from 0 to 32127
- slot_of: int32 [16], replicated, may hold values from 0 to 15, each once
- lengths: int32 [16], replicated, may hold values from 257 to 1024, as said below
- block_table: int32 [16, 8], replicated, may hold values from 0 to 127, as said below
- kv_pool: bfloat16 [2, 128, 128, 2048], P(None, None, 'dev', 'section'), may hold values from -30 to 30
- self_cache: bfloat16 [2, 16, 128, 2048], P(None, 'dev', None, 'section'), may hold values from -30 to 30
- embedding: bfloat16 [32128, 4096], P(None, 'dev'), may hold values from -30 to 30
- norm_self: float32 [4096], P('dev'), may hold values from 0.25 to 1.75
- norm_cross: float32 [4096], P('dev'), may hold values from 0.25 to 1.75
- norm_ffn: float32 [4096], P('dev'), may hold values from 0.25 to 1.75
- w_self_qkv: bfloat16 [4096, 3, 2048], P('dev', None, 'section'), may hold values from -0.09375 to 0.09375
- w_self_out: bfloat16 [2048, 4096], P('section', 'dev'), may hold values from -0.125 to 0.125
- w_cross_q: bfloat16 [4096, 2048], P('dev', 'section'), may hold values from -0.09375 to 0.09375
- w_cross_out: bfloat16 [2048, 4096], P('section', 'dev'), may hold values from -0.125 to 0.125
- w_in: bfloat16 [4096, 2, 5120], P('dev', None, 'section'), may hold values from -0.09375 to 0.09375
- w_out: bfloat16 [5120, 4096], P('section', 'dev'), may hold values from -0.078125 to 0.078125
Outputs:
- out: bfloat16 [1, 16, 4096], P(None, None, 'dev')
The draws below stay inside these ranges and needn't reach their ends.
Inputs may be any that keep to these rules, and one draw needn't show every extreme that they name: A permutation: request r occupies decoder slot slot_of[r]. `lengths`: one request has exactly 1024 source tokens. `block_table`: all entries differ.
All inputs are finite; a program needn't handle non-finite values.
Results may differ from the reference program's by a relative error of at most 0.008.
Values may be sent and summed in bfloat16 or wider, within the bound.
A program may use at most 128 MiB of HBM per device.

```python
import math
import jax
import jax.numpy as jnp
import numpy as np
from jax import lax

D = 4096
DH = 64
VOCAB = 32128
HEADS = 32
FF = 5120
BLOCK = 128
MAXB = 8
STEPS = 1
PREV = 128
INNER = 2048
REQ = 16
POOL = 128


def paired_keys(key, lead, rows, width, low, high, share):
    k_first, k_second, k_pick, k_boost = jax.random.split(key, 4)
    first = jax.random.normal(k_first, (lead, rows // 2, 1, width))
    noise = jax.random.normal(k_second, (lead, rows // 2, 1, width))
    second = noise
    pairs = jnp.concatenate([first, second], axis=2)
    chosen = jax.random.uniform(k_pick, (lead, rows // 2, 1, 1)) < share
    boost = jnp.exp(jax.random.uniform(k_boost, (lead, rows // 2, 1, 1), minval=math.log(low), maxval=math.log(high)))
    factor = jnp.where(chosen, boost, 1.0)
    return (pairs * factor).reshape(lead, rows, width)


def draw_kv_pool(key, part):
    key = jax.random.fold_in(key, 11)
    k_keys, k_values = jax.random.split(key)
    keys = paired_keys(k_keys, POOL, BLOCK, INNER, 1.0, 1.0, 0.0)
    values = jax.random.normal(k_values, (POOL, BLOCK, INNER))
    return jnp.clip(jnp.stack([keys, values]), -30.0, 30.0).astype(jnp.bfloat16)


def draw_self_cache(key, part):
    key = jax.random.fold_in(key, 12)
    k_keys, k_values = jax.random.split(key)
    keys = paired_keys(k_keys, REQ, PREV, INNER, 1.0, 1.0, 0.0)
    values = jax.random.normal(k_values, (REQ, PREV, INNER))
    return jnp.clip(jnp.stack([keys, values]), -30.0, 30.0).astype(jnp.bfloat16)


def draw_lengths(key, part):
    key = jax.random.fold_in(key, 13)
    k_one, k_two, k_three, k_extra, k_long = jax.random.split(key, 5)
    blocks = jnp.minimum(jax.random.randint(k_one, (REQ,), 3, MAXB + 1), jax.random.randint(k_two, (REQ,), 3, MAXB + 1))
    blocks = jnp.minimum(blocks, jax.random.randint(k_three, (REQ,), 3, MAXB + 1))
    extra = jax.random.randint(k_extra, (REQ,), 1, BLOCK + 1)
    longest = jax.random.randint(k_long, (), 0, REQ)
    sizes = (blocks - 1) * BLOCK + extra
    return jnp.where(jnp.arange(REQ) == longest, MAXB * BLOCK, sizes).astype(jnp.int32)


def draw_block_table(key, part):
    key = jax.random.fold_in(key, 14)
    return jax.random.permutation(key, POOL).reshape(REQ, MAXB).astype(jnp.int32)


def embed_rows(key, low_spread, row_spread, base):
    k_col, k_row = jax.random.split(key)
    rise = jnp.arange(D, dtype=jnp.float32) / D
    column = jnp.exp(math.log(10.0) * (low_spread * rise + (1.0 - low_spread) * jax.random.uniform(k_col, (D,))))
    row = jnp.exp(math.log(row_spread) * jax.random.uniform(k_row, (VOCAB, 1)))
    return jnp.clip(0.3 * base * column[None, :] * row, -30.0, 30.0)


def draw_embedding(key, part):
    key = jax.random.fold_in(key, 15)
    k_base, k_scale = jax.random.split(key)
    base = jnp.clip(jax.random.normal(k_base, (VOCAB, D)), -6.0, 6.0)
    return embed_rows(k_scale, 0.5, 3.0, base).astype(jnp.bfloat16)


def set_ends(values, own_key, smallest, largest):
    dims = values.shape
    place = [jax.random.randint(jax.random.fold_in(own_key, axis), (), 0, dims[axis]) for axis in range(len(dims))]
    values = values.at[tuple(place)].set(smallest)
    longest = dims.index(max(dims))
    place[longest] = (place[longest] + 1) % dims[longest]
    return values.at[tuple(place)].set(largest)


def level_of(rng, dims, cuts, least, top_value):
    loudness, own = 1.0, jax.random.fold_in(rng, 6)
    for dim, shards_of in cuts:
        heights = jnp.exp(jax.random.uniform(jax.random.fold_in(own, dim), (shards_of,), jnp.float32, least / len(cuts), top_value / len(cuts)))
        loudness = loudness * jnp.repeat(heights, dims[dim] // shards_of).reshape([-1 if axis == dim else 1 for axis in range(len(dims))])
    return loudness


def cumulative_ranks(amount, lean):
    portions = [(1 << 20) // math.isqrt(standing ** lean) + 1 for standing in range(1, amount + 1)]
    spread = 1 + sum(portions) // (1 << 30)
    return np.cumsum(np.array([max(1, weight // spread) for weight in portions]))


def skewed_ids(rng, extent, count, skew):
    grid = cumulative_ranks(count, skew)
    ticket = jax.random.randint(jax.random.fold_in(rng, 1), extent, 0, int(grid[count - 1]))
    standing = jnp.searchsorted(jnp.asarray(grid, jnp.int32), ticket, side="right")
    return jax.random.permutation(jax.random.fold_in(rng, 2), count)[standing].astype(jnp.int32)


def bell_draw(stream_key, dims, scale, limit, cuts=(), held_as=jnp.bfloat16):
    entries = scale * jax.random.normal(stream_key, dims, jnp.float32)
    if cuts:
        entries = entries * level_of(stream_key, dims, cuts, -0.22, 0.18)
    return jnp.clip(entries, -limit, limit).astype(held_as)


def setup_inputs(seed: int = 0) -> dict:
    seeds = jax.random.split(jax.random.key(seed), 17)
    token_ids = set_ends(skewed_ids(seeds[0], (STEPS, REQ), VOCAB, 2), jax.random.fold_in(seeds[0], 3), 0, VOCAB - 1).astype(jnp.int32)
    slot_of = jax.random.permutation(seeds[1], REQ).astype(jnp.int32)
    lengths = draw_lengths(jax.random.fold_in(seeds[16], 71), 0)
    block_table = draw_block_table(jax.random.fold_in(seeds[16], 71), 0)
    kv_pool = draw_kv_pool(jax.random.fold_in(seeds[16], 71), 0)
    self_cache = draw_self_cache(jax.random.fold_in(seeds[16], 71), 0)
    embedding = draw_embedding(jax.random.fold_in(seeds[16], 71), 0)
    norm_self = jnp.clip(1.0 + 0.15 * jax.random.normal(seeds[7], (D,), jnp.float32), 0.25, 1.75)
    norm_cross = jnp.clip(1.0 + 0.15 * jax.random.normal(seeds[8], (D,), jnp.float32), 0.25, 1.75)
    norm_ffn = jnp.clip(1.0 + 0.15 * jax.random.normal(seeds[9], (D,), jnp.float32), 0.25, 1.75)
    w_self_qkv = bell_draw(seeds[10], (D, 3, INNER), D ** -0.5, 0.09375, ((0, 16), (2, 2)))
    w_self_out = bell_draw(seeds[11], (INNER, D), INNER ** -0.5, 0.125, ((0, 2), (1, 16)))
    w_cross_q = bell_draw(seeds[12], (D, INNER), D ** -0.5, 0.09375, ((0, 16), (1, 2)))
    w_cross_out = bell_draw(seeds[13], (INNER, D), INNER ** -0.5, 0.125, ((0, 2), (1, 16)))
    w_in = bell_draw(seeds[14], (D, 2, FF), D ** -0.5, 0.09375, ((0, 16), (2, 2)))
    w_out = bell_draw(seeds[15], (FF, D), FF ** -0.5, 0.078125, ((0, 2), (1, 16)))
    return dict(token_ids=token_ids, slot_of=slot_of, lengths=lengths, block_table=block_table, kv_pool=kv_pool, self_cache=self_cache, embedding=embedding, norm_self=norm_self, norm_cross=norm_cross, norm_ffn=norm_ffn, w_self_qkv=w_self_qkv, w_self_out=w_self_out, w_cross_q=w_cross_q, w_cross_out=w_cross_out, w_in=w_in, w_out=w_out)


EPS = 1e-06

def rms_norm(resid, gain):
    scale = lax.rsqrt(lax.optimization_barrier(jnp.mean(resid * resid, axis=1, keepdims=True)) + EPS)
    return (resid * scale * gain[None, :]).astype(jnp.bfloat16)

def attend(query, keys, values, valid):
    scores = jnp.einsum('rhe,rjhe->rhj', query.astype(jnp.float32), keys.astype(jnp.float32))
    mask = valid[:, None, :]
    top = lax.optimization_barrier(jnp.max(jnp.where(mask, scores, -jnp.inf), axis=2, keepdims=True))
    weights = jnp.where(mask, jnp.exp(jnp.where(mask, scores, top) - top), 0.0)
    total = lax.optimization_barrier(jnp.sum(weights, axis=2))
    rounded = lax.optimization_barrier(weights.astype(jnp.bfloat16))
    mixed = jnp.einsum('rhj,rjhe->rhe', rounded.astype(jnp.float32), values.astype(jnp.float32))
    return (mixed / total[:, :, None]).astype(jnp.bfloat16)

def reference(token_ids, slot_of, lengths, block_table, kv_pool, self_cache, embedding, norm_self, norm_cross, norm_ffn, w_self_qkv, w_self_out, w_cross_q, w_cross_out, w_in, w_out):
    requests = slot_of.shape[0]
    cache = self_cache[:, slot_of]
    count = PREV + STEPS
    new_keys = jnp.zeros((requests, STEPS, INNER), jnp.bfloat16)
    new_values = jnp.zeros((requests, STEPS, INNER), jnp.bfloat16)

    def cross_one(items):
        query, table, length = items
        rows = kv_pool[:, table]
        keys = rows[0].reshape(1, MAXB * BLOCK, HEADS, DH)
        values = rows[1].reshape(1, MAXB * BLOCK, HEADS, DH)
        valid = (jnp.arange(MAXB * BLOCK) < length)[None, :]
        return attend(query[None], keys, values, valid)[0]
    outputs = []
    for step in range(STEPS):
        resid = embedding[token_ids[step]].astype(jnp.float32)
        normed = rms_norm(resid, norm_self)
        qkv = jnp.dot(normed, w_self_qkv.reshape(D, 3 * INNER), preferred_element_type=jnp.float32)
        qkv = qkv.astype(jnp.bfloat16).reshape(requests, 3, INNER)
        new_keys = new_keys.at[:, step].set(qkv[:, 1])
        new_values = new_values.at[:, step].set(qkv[:, 2])
        keys = jnp.concatenate([cache[0], new_keys], axis=1).reshape(requests, count, HEADS, DH)
        values = jnp.concatenate([cache[1], new_values], axis=1).reshape(requests, count, HEADS, DH)
        valid = jnp.broadcast_to(jnp.arange(count) < PREV + step + 1, (requests, count))
        mixed = attend(qkv[:, 0].reshape(requests, HEADS, DH), keys, values, valid)
        resid = resid + jnp.dot(mixed.reshape(requests, INNER), w_self_out, preferred_element_type=jnp.float32)
        normed = rms_norm(resid, norm_cross)
        query = jnp.dot(normed, w_cross_q, preferred_element_type=jnp.float32).astype(jnp.bfloat16)
        mixed = lax.map(cross_one, (query.reshape(requests, HEADS, DH), block_table, lengths))
        resid = resid + jnp.dot(mixed.reshape(requests, INNER), w_cross_out, preferred_element_type=jnp.float32)
        normed = rms_norm(resid, norm_ffn)
        gated = jnp.dot(normed, w_in.reshape(D, 2 * FF), preferred_element_type=jnp.float32).reshape(requests, 2, FF)
        hidden = (jax.nn.gelu(gated[:, 0], approximate=True) * gated[:, 1]).astype(jnp.bfloat16)
        resid = resid + jnp.dot(hidden, w_out, preferred_element_type=jnp.float32)
        outputs.append(resid.astype(jnp.bfloat16))
    return jnp.stack(outputs)
```

```python
import jax
import jax.numpy as jnp
from jax import lax
from jax.sharding import PartitionSpec as P

DH = 64
EPS = 1e-06
LANES = 128


def project(resid, gain, weight):
    width = resid.shape[1] * lax.axis_size("dev")
    scaled = (resid * gain[None, :]).astype(jnp.bfloat16)
    part = jnp.dot(scaled, weight, preferred_element_type=jnp.float32)
    squares = jnp.sum(resid * resid, axis=1, keepdims=True)
    packed = jnp.concatenate([part, jnp.broadcast_to(squares, (resid.shape[0], LANES))], axis=1)
    total = lax.psum(packed, "dev")
    scale = lax.rsqrt(total[:, -1:] / width + EPS)
    return total[:, :-LANES] * scale


def output(active, weight):
    return lax.psum(jnp.dot(active, weight, preferred_element_type=jnp.float32), "section")


def own_rows(array, own):
    return lax.dynamic_slice_in_dim(array, lax.axis_index("dev") * own, own, 0)


def self_attend(query, key, value, cache):
    own, features = query.shape
    heads = features // DH
    pick = (jnp.arange(features)[:, None] // DH == jnp.arange(heads)[None, :])
    spread = jnp.where(pick[None], query[:, :, None], 0).astype(jnp.bfloat16)
    scores = jnp.einsum("rjf,rfh->rjh", cache[0], spread, preferred_element_type=jnp.float32)
    fresh = jnp.sum(
        (query.astype(jnp.float32) * key.astype(jnp.float32)).reshape(own, heads, DH), axis=2
    )
    top = jnp.maximum(jnp.max(scores, axis=1), fresh)
    weights = jnp.exp(scores - top[:, None, :])
    weight = jnp.exp(fresh - top)
    total = jnp.sum(weights, axis=1) + weight
    mixed = jnp.einsum(
        "rjh,rjf->rhf", weights.astype(jnp.bfloat16), cache[1], preferred_element_type=jnp.float32
    )
    mixed = jnp.sum(jnp.where(pick.T[None], mixed, 0.0), axis=1)
    wide = jnp.repeat(weight.astype(jnp.bfloat16).astype(jnp.float32), DH, axis=1)
    mixed = mixed + wide * value.astype(jnp.float32)
    return (mixed / jnp.repeat(total, DH, axis=1)).astype(jnp.bfloat16)


def cross_attend(query, pool, owner, valid):
    requests, features = query.shape
    heads = features // DH
    pick = (jnp.arange(features)[:, None] // DH == jnp.arange(heads)[None, :])
    spread = jnp.where(pick.T[None], query[:, None, :], 0).reshape(requests * heads, features)
    scores = lax.dot_general(
        spread, pool[0], (((1,), (1,)), ((), ())), preferred_element_type=jnp.float32
    )
    column = jnp.arange(requests * heads) // heads
    mask = (column[:, None] == owner[None, :]) & valid[None, :]
    top = lax.pmax(jnp.max(jnp.where(mask, scores, -jnp.inf), axis=1), "dev")[:, None]
    weights = jnp.where(mask, jnp.exp(jnp.where(mask, scores, top) - top), 0.0)
    total = jnp.sum(weights, axis=1).reshape(requests, heads)
    mixed = jnp.dot(weights.astype(jnp.bfloat16), pool[1], preferred_element_type=jnp.float32)
    mixed = jnp.sum(
        jnp.where(pick.T[None], mixed.reshape(requests, heads, features), 0.0), axis=1
    )
    packed = jnp.concatenate([mixed, jnp.pad(total, ((0, 0), (0, -heads % LANES)))], axis=1)
    packed = lax.psum(packed, "dev")
    total = packed[:, features : features + heads]
    return (packed[:, :features] / jnp.repeat(total, DH, axis=1)).astype(jnp.bfloat16)


def local(
    token_ids,
    slot_of,
    lengths,
    block_table,
    kv_pool,
    self_cache,
    embedding,
    norm_self,
    norm_cross,
    norm_ffn,
    w_self_qkv,
    w_self_out,
    w_cross_q,
    w_cross_out,
    w_in,
    w_out,
):
    dev_count = lax.axis_size("dev")
    requests, max_blocks = block_table.shape
    own = requests // dev_count
    half_inner = w_cross_q.shape[1]
    here = lax.axis_index("dev")
    blocks, rows_here = kv_pool.shape[1:3]
    block_rows = rows_here * dev_count

    slot_hot = slot_of[:, None] == jnp.arange(requests)[None, :]
    ids_slot = jnp.sum(jnp.where(slot_hot, token_ids[0][:, None], 0), axis=0)

    place = slot_of[:, None] * max_blocks + jnp.arange(max_blocks)[None, :] + 1
    hit = block_table.reshape(-1)[:, None] == jnp.arange(blocks)[None, :]
    holder = jnp.sum(jnp.where(hit, place.reshape(-1)[:, None], 0), axis=0) - 1
    span = jnp.sum(jnp.where(hit, jnp.repeat(lengths, max_blocks)[:, None], 0), axis=0)
    first = (holder % max_blocks) * block_rows + here * rows_here
    valid = (first[:, None] + jnp.arange(rows_here)[None, :] < span[:, None]).reshape(-1)
    owner = jnp.repeat(jnp.where(holder >= 0, holder // max_blocks, -1), rows_here)
    pool = kv_pool.reshape(2, blocks * rows_here, half_inner)

    resid = embedding[ids_slot].astype(jnp.float32)
    qkv = project(resid, norm_self, w_self_qkv.reshape(w_self_qkv.shape[0], -1))
    qkv = own_rows(qkv, own).astype(jnp.bfloat16).reshape(own, 3, half_inner)
    mixed = self_attend(qkv[:, 0], qkv[:, 1], qkv[:, 2], self_cache)
    mixed = lax.all_gather(mixed, "dev", axis=0, tiled=True)
    resid = resid + output(mixed, w_self_out)

    query = project(resid, norm_cross, w_cross_q).astype(jnp.bfloat16)
    mixed = cross_attend(query, pool, owner, valid)
    resid = resid + output(mixed, w_cross_out)

    gated = own_rows(project(resid, norm_ffn, w_in.reshape(w_in.shape[0], -1)), own)
    gated = gated.reshape(own, 2, -1)
    hidden = (jax.nn.gelu(gated[:, 0], approximate=True) * gated[:, 1]).astype(jnp.bfloat16)
    hidden = lax.all_gather(hidden, "dev", axis=0, tiled=True)
    resid = resid + output(hidden, w_out)
    out = jnp.dot(
        slot_hot.astype(jnp.bfloat16), resid.astype(jnp.bfloat16), preferred_element_type=jnp.float32
    )
    return out.astype(jnp.bfloat16)[None]


def solution(mesh):
    in_specs = (
        P(),
        P(),
        P(),
        P(),
        P(None, None, "dev", "section"),
        P(None, "dev", None, "section"),
        P(None, "dev"),
        P("dev"),
        P("dev"),
        P("dev"),
        P("dev", None, "section"),
        P("section", "dev"),
        P("dev", "section"),
        P("section", "dev"),
        P("dev", None, "section"),
        P("section", "dev"),
    )
    out_specs = P(None, None, "dev")
    return jax.shard_map(local, mesh=mesh, in_specs=in_specs, out_specs=out_specs, check_vma=False)
```

```python
import functools

import jax
import jax.numpy as jnp
from jax import lax
from jax.experimental import pallas as pl
from jax.experimental.pallas import tpu as pltpu
from jax.sharding import PartitionSpec as P

DH = 64
EPS = 1e-06
LANES = 128
LOWEST = -1e30


def exchange_kernel(n, scatter, spread, combine, x_ref, out_ref, *scratch):
    scratch = list(scratch)
    me = lax.axis_index("dev")
    section = lax.axis_index("section")

    def peer(step):
        return (section, lax.rem(me + step, n))

    barrier = pltpu.get_barrier_semaphore()

    @pl.loop(1, n)
    def _(step):
        pl.semaphore_signal(barrier, inc=1, device_id=peer(step), device_id_type=pl.DeviceIdType.MESH)

    pl.semaphore_wait(barrier, n - 1)

    if scatter:
        held, sent, got = scratch[:3]
        scratch = scratch[3:]

        def chunk(step):
            return pltpu.make_async_remote_copy(
                src_ref=x_ref.at[lax.rem(me + step, n)],
                dst_ref=held.at[step],
                send_sem=sent.at[step],
                recv_sem=got.at[step],
                device_id=peer(step),
                device_id_type=pl.DeviceIdType.MESH,
            )

        @pl.loop(1, n)
        def _(step):
            chunk(step).start()

        held[0] = x_ref[me]

        @pl.loop(1, n)
        def _(step):
            chunk(step).wait()

        result = combine(held)
    else:
        result = combine(x_ref)

    if not spread:
        out_ref[...] = result
        return
    mine, full, sent, got = scratch
    mine[...] = result

    def row(step):
        return pltpu.make_async_remote_copy(
            src_ref=mine,
            dst_ref=full.at[me],
            send_sem=sent.at[step],
            recv_sem=got.at[step],
            device_id=peer(step),
            device_id_type=pl.DeviceIdType.MESH,
        )

    @pl.loop(1, n)
    def _(step):
        row(step).start()

    full[me] = result

    @pl.loop(1, n)
    def _(step):
        row(step).wait()

    out_ref[...] = full[...]


def exchange(x, columns, combine, collective_id, scatter=True, spread=True):
    n = lax.axis_size("dev")
    own = x.shape[0] // n if scatter else x.shape[0]
    width = x.shape[1]
    scratch = []
    if scatter:
        x = x.reshape(n, own, width)
        scratch += [pltpu.VMEM((n, own, width), jnp.float32)] + [pltpu.SemaphoreType.DMA((n,))] * 2
    if spread:
        scratch += [pltpu.VMEM((own, columns), jnp.float32), pltpu.VMEM((n, own, columns), jnp.float32)]
        scratch += [pltpu.SemaphoreType.DMA((n,))] * 2
    result = pl.pallas_call(
        functools.partial(exchange_kernel, n, scatter, spread, combine),
        out_shape=jax.ShapeDtypeStruct((n, own, columns) if spread else (own, columns), jnp.float32),
        in_specs=[pl.BlockSpec(memory_space=pltpu.VMEM)],
        out_specs=pl.BlockSpec(memory_space=pltpu.VMEM),
        scratch_shapes=scratch,
        compiler_params=pltpu.CompilerParams(
            collective_id=collective_id, has_side_effects=True, vmem_limit_bytes=48 * 1024 * 1024
        ),
    )(x)
    return result.reshape(-1, columns)


def scaled_sum(width, held):
    total = jnp.sum(held[...], axis=0)
    squares = jnp.max(total[:, -LANES:], axis=1, keepdims=True)
    return total[:, :-LANES] * lax.rsqrt(squares / width + EPS)


def gated_sum(width, held):
    gated = scaled_sum(width, held)
    units = gated.shape[1] // 2
    gate = gated[:, :units]
    bent = 0.7978845608028654 * (gate + 0.044715 * (gate * gate * gate))
    return 0.5 * gate * (1.0 + jnp.tanh(bent)) * gated[:, units:]


def merged(features, held):
    parts = held[...]
    mixed, top, total = (parts[:, :, i * features : (i + 1) * features] for i in range(3))
    factor = jnp.exp(top - jnp.max(top, axis=0)[None])
    return jnp.sum(factor * mixed, axis=0) / jnp.sum(factor * total, axis=0)


def unchanged(ref):
    return ref[...]


def project(resid, gain, weight):
    scaled = (resid * gain[None, :]).astype(jnp.bfloat16)
    part = jnp.dot(scaled, weight, preferred_element_type=jnp.float32)
    squares = jnp.sum(resid * resid, axis=1, keepdims=True)
    return jnp.concatenate([part, jnp.broadcast_to(squares, (resid.shape[0], LANES))], axis=1)


def output(active, weight):
    return lax.psum(jnp.dot(active, weight, preferred_element_type=jnp.float32), "section")


def self_attend(query, key, value, cache):
    own, features = query.shape
    heads = features // DH
    pick = (jnp.arange(features)[:, None] // DH == jnp.arange(heads)[None, :])
    spread = jnp.where(pick[None], query[:, :, None], 0).astype(jnp.bfloat16)
    scores = jnp.einsum("rjf,rfh->rjh", cache[0], spread, preferred_element_type=jnp.float32)
    fresh = jnp.sum(
        (query.astype(jnp.float32) * key.astype(jnp.float32)).reshape(own, heads, DH), axis=2
    )
    top = jnp.maximum(jnp.max(scores, axis=1), fresh)
    weights = jnp.exp(scores - top[:, None, :])
    weight = jnp.exp(fresh - top)
    total = jnp.sum(weights, axis=1) + weight
    mixed = jnp.einsum(
        "rjh,rjf->rhf", weights.astype(jnp.bfloat16), cache[1], preferred_element_type=jnp.float32
    )
    mixed = jnp.sum(jnp.where(pick.T[None], mixed, 0.0), axis=1)
    wide = jnp.repeat(weight.astype(jnp.bfloat16).astype(jnp.float32), DH, axis=1)
    mixed = mixed + wide * value.astype(jnp.float32)
    return (mixed / jnp.repeat(total, DH, axis=1)).astype(jnp.bfloat16)


def cross_attend(query, pool, owner, valid):
    requests, features = query.shape
    heads = features // DH
    pick = (jnp.arange(features)[:, None] // DH == jnp.arange(heads)[None, :])
    spread = jnp.where(pick.T[None], query[:, None, :], 0).reshape(requests * heads, features)
    scores = lax.dot_general(
        spread, pool[0], (((1,), (1,)), ((), ())), preferred_element_type=jnp.float32
    )
    column = jnp.arange(requests * heads) // heads
    mask = (column[:, None] == owner[None, :]) & valid[None, :]
    top = jnp.max(jnp.where(mask, scores, LOWEST), axis=1, keepdims=True)
    weights = jnp.where(mask, jnp.exp(jnp.where(mask, scores, top) - top), 0.0)
    total = jnp.sum(weights, axis=1).reshape(requests, heads)
    mixed = jnp.dot(weights.astype(jnp.bfloat16), pool[1], preferred_element_type=jnp.float32)
    mixed = jnp.sum(
        jnp.where(pick.T[None], mixed.reshape(requests, heads, features), 0.0), axis=1
    )
    top = jnp.repeat(top.reshape(requests, heads), DH, axis=1)
    packed = jnp.concatenate([mixed, top, jnp.repeat(total, DH, axis=1)], axis=1)
    return exchange(packed, features, functools.partial(merged, features), 3).astype(jnp.bfloat16)


def local(
    token_ids,
    slot_of,
    lengths,
    block_table,
    kv_pool,
    self_cache,
    embedding,
    norm_self,
    norm_cross,
    norm_ffn,
    w_self_qkv,
    w_self_out,
    w_cross_q,
    w_cross_out,
    w_in,
    w_out,
):
    dev_count = lax.axis_size("dev")
    requests, max_blocks = block_table.shape
    own = requests // dev_count
    half_inner = w_cross_q.shape[1]
    here = lax.axis_index("dev")
    blocks, rows_here = kv_pool.shape[1:3]
    block_rows = rows_here * dev_count

    slot_hot = slot_of[:, None] == jnp.arange(requests)[None, :]
    ids_slot = jnp.sum(jnp.where(slot_hot, token_ids[0][:, None], 0), axis=0)

    place = slot_of[:, None] * max_blocks + jnp.arange(max_blocks)[None, :] + 1
    hit = block_table.reshape(-1)[:, None] == jnp.arange(blocks)[None, :]
    holder = jnp.sum(jnp.where(hit, place.reshape(-1)[:, None], 0), axis=0) - 1
    span = jnp.sum(jnp.where(hit, jnp.repeat(lengths, max_blocks)[:, None], 0), axis=0)
    first = (holder % max_blocks) * block_rows + here * rows_here
    valid = (first[:, None] + jnp.arange(rows_here)[None, :] < span[:, None]).reshape(-1)
    owner = jnp.repeat(jnp.where(holder >= 0, holder // max_blocks, -1), rows_here)
    pool = kv_pool.reshape(2, blocks * rows_here, half_inner)

    resid = embedding[ids_slot].astype(jnp.float32)
    width = resid.shape[1] * dev_count
    summed = functools.partial(scaled_sum, width)
    qkv = project(resid, norm_self, w_self_qkv.reshape(w_self_qkv.shape[0], -1))
    qkv = exchange(qkv, 3 * half_inner, summed, 0, spread=False)
    qkv = qkv.astype(jnp.bfloat16).reshape(own, 3, half_inner)
    mixed = self_attend(qkv[:, 0], qkv[:, 1], qkv[:, 2], self_cache).astype(jnp.float32)
    mixed = exchange(mixed, half_inner, unchanged, 1, scatter=False).astype(jnp.bfloat16)
    resid = resid + output(mixed, w_self_out)

    query = exchange(project(resid, norm_cross, w_cross_q), half_inner, summed, 2)
    mixed = cross_attend(query.astype(jnp.bfloat16), pool, owner, valid)
    resid = resid + output(mixed, w_cross_out)

    gated = project(resid, norm_ffn, w_in.reshape(w_in.shape[0], -1))
    hidden = exchange(gated, w_in.shape[2], functools.partial(gated_sum, width), 4)
    resid = resid + output(hidden.astype(jnp.bfloat16), w_out)
    out = jnp.dot(
        slot_hot.astype(jnp.bfloat16), resid.astype(jnp.bfloat16), preferred_element_type=jnp.float32
    )
    return out.astype(jnp.bfloat16)[None]


def solution(mesh):
    in_specs = (
        P(),
        P(),
        P(),
        P(),
        P(None, None, "dev", "section"),
        P(None, "dev", None, "section"),
        P(None, "dev"),
        P("dev"),
        P("dev"),
        P("dev"),
        P("dev", None, "section"),
        P("section", "dev"),
        P("dev", "section"),
        P("section", "dev"),
        P("dev", None, "section"),
        P("section", "dev"),
    )
    out_specs = P(None, None, "dev")
    return jax.shard_map(local, mesh=mesh, in_specs=in_specs, out_specs=out_specs, check_vma=False)
```

```python
import functools

import jax
import jax.numpy as jnp
from jax import lax
from jax.experimental import pallas as pl
from jax.experimental.pallas import tpu as pltpu
from jax.sharding import PartitionSpec as P

DH = 64
EPS = 1e-06
LANES = 128
LOWEST = -1e30


def exchange_kernel(n, scatter, spread, combine, x_ref, out_ref, *scratch):
    scratch = list(scratch)
    me = lax.axis_index("dev")
    section = lax.axis_index("section")

    def peer(step):
        return (section, lax.rem(me + step, n))

    barrier = pltpu.get_barrier_semaphore()

    @pl.loop(1, n)
    def _(step):
        pl.semaphore_signal(barrier, inc=1, device_id=peer(step), device_id_type=pl.DeviceIdType.MESH)

    pl.semaphore_wait(barrier, n - 1)

    if scatter:
        held, sent, got = scratch[:3]
        scratch = scratch[3:]

        def chunk(step):
            return pltpu.make_async_remote_copy(
                src_ref=x_ref.at[lax.rem(me + step, n)],
                dst_ref=held.at[step],
                send_sem=sent.at[step],
                recv_sem=got.at[step],
                device_id=peer(step),
                device_id_type=pl.DeviceIdType.MESH,
            )

        @pl.loop(1, n)
        def _(step):
            chunk(step).start()

        held[0] = x_ref[me]

        @pl.loop(1, n)
        def _(step):
            chunk(step).wait()

        result = combine(held)
    else:
        result = combine(x_ref)

    if not spread:
        out_ref[...] = result
        return
    mine, full, sent, got = scratch
    mine[...] = result

    def row(step):
        return pltpu.make_async_remote_copy(
            src_ref=mine,
            dst_ref=full.at[me],
            send_sem=sent.at[step],
            recv_sem=got.at[step],
            device_id=peer(step),
            device_id_type=pl.DeviceIdType.MESH,
        )

    @pl.loop(1, n)
    def _(step):
        row(step).start()

    full[me] = result

    @pl.loop(1, n)
    def _(step):
        row(step).wait()

    out_ref[...] = full[...]


def exchange(x, columns, combine, collective_id, scatter=True, spread=True):
    n = lax.axis_size("dev")
    own = x.shape[0] // n if scatter else x.shape[0]
    width = x.shape[1]
    scratch = []
    if scatter:
        x = x.reshape(n, own, width)
        scratch += [pltpu.VMEM((n, own, width), jnp.float32)] + [pltpu.SemaphoreType.DMA((n,))] * 2
    if spread:
        scratch += [pltpu.VMEM((own, columns), jnp.float32), pltpu.VMEM((n, own, columns), jnp.float32)]
        scratch += [pltpu.SemaphoreType.DMA((n,))] * 2
    result = pl.pallas_call(
        functools.partial(exchange_kernel, n, scatter, spread, combine),
        out_shape=jax.ShapeDtypeStruct((n, own, columns) if spread else (own, columns), jnp.float32),
        in_specs=[pl.BlockSpec(memory_space=pltpu.VMEM)],
        out_specs=pl.BlockSpec(memory_space=pltpu.VMEM),
        scratch_shapes=scratch,
        compiler_params=pltpu.CompilerParams(
            collective_id=collective_id, has_side_effects=True, vmem_limit_bytes=48 * 1024 * 1024
        ),
    )(x)
    return result.reshape(-1, columns)


def scaled_sum(width, held):
    total = jnp.sum(held[...], axis=0)
    squares = jnp.max(total[:, -LANES:], axis=1, keepdims=True)
    return total[:, :-LANES] * lax.rsqrt(squares / width + EPS)


def gated_sum(width, held):
    gated = scaled_sum(width, held)
    units = gated.shape[1] // 2
    gate = gated[:, :units]
    bent = 0.7978845608028654 * (gate + 0.044715 * (gate * gate * gate))
    return 0.5 * gate * (1.0 + jnp.tanh(bent)) * gated[:, units:]


def merged(features, held):
    parts = held[...]
    mixed, top, total = (parts[:, :, i * features : (i + 1) * features] for i in range(3))
    factor = jnp.exp(top - jnp.max(top, axis=0)[None])
    return jnp.sum(factor * mixed, axis=0) / jnp.sum(factor * total, axis=0)


def unchanged(ref):
    return ref[...]


def project(resid, gain, weight):
    scaled = (resid * gain[None, :]).astype(jnp.bfloat16)
    part = jnp.dot(scaled, weight, preferred_element_type=jnp.float32)
    squares = jnp.sum(resid * resid, axis=1, keepdims=True)
    return jnp.concatenate([part, jnp.broadcast_to(squares, (resid.shape[0], LANES))], axis=1)


def embed_kernel(window, ids_ref, table_ref, out_ref, held, sem):
    requests = out_ref.shape[0]

    def fetch(index):
        first = pl.multiple_of(ids_ref[index] // window * window, window)
        return pltpu.make_async_copy(
            table_ref.at[pl.ds(first, window)], held.at[index], sem.at[index]
        )

    @pl.loop(0, requests)
    def _(index):
        fetch(index).start()

    @pl.loop(0, requests)
    def _(index):
        fetch(index).wait()
        rows = held[index].astype(jnp.float32)
        here = lax.broadcasted_iota(jnp.int32, rows.shape, 0) == ids_ref[index] % window
        out_ref[pl.ds(index, 1)] = jnp.sum(jnp.where(here, rows, 0.0), axis=0, keepdims=True)


def embed(ids, table):
    window = 16
    requests, width = ids.shape[0], table.shape[1]
    if table.shape[0] % window:
        return table[ids].astype(jnp.float32)
    return pl.pallas_call(
        functools.partial(embed_kernel, window),
        out_shape=jax.ShapeDtypeStruct((requests, width), jnp.float32),
        in_specs=[pl.BlockSpec(memory_space=pltpu.SMEM), pl.BlockSpec(memory_space=pl.ANY)],
        out_specs=pl.BlockSpec(memory_space=pltpu.VMEM),
        scratch_shapes=[
            pltpu.VMEM((requests, window, width), table.dtype),
            pltpu.SemaphoreType.DMA((requests,)),
        ],
    )(ids, table)


def output(active, weight):
    return lax.psum(jnp.dot(active, weight, preferred_element_type=jnp.float32), "section")


def self_attend(query, key, value, cache):
    own, features = query.shape
    heads = features // DH
    pick = (jnp.arange(features)[:, None] // DH == jnp.arange(heads)[None, :])
    spread = jnp.where(pick[None], query[:, :, None], 0).astype(jnp.bfloat16)
    scores = jnp.einsum("rjf,rfh->rjh", cache[0], spread, preferred_element_type=jnp.float32)
    fresh = jnp.sum(
        (query.astype(jnp.float32) * key.astype(jnp.float32)).reshape(own, heads, DH), axis=2
    )
    top = jnp.maximum(jnp.max(scores, axis=1), fresh)
    weights = jnp.exp(scores - top[:, None, :])
    weight = jnp.exp(fresh - top)
    total = jnp.sum(weights, axis=1) + weight
    mixed = jnp.einsum(
        "rjh,rjf->rhf", weights.astype(jnp.bfloat16), cache[1], preferred_element_type=jnp.float32
    )
    mixed = jnp.sum(jnp.where(pick.T[None], mixed, 0.0), axis=1)
    wide = jnp.repeat(weight.astype(jnp.bfloat16).astype(jnp.float32), DH, axis=1)
    mixed = mixed + wide * value.astype(jnp.float32)
    return (mixed / jnp.repeat(total, DH, axis=1)).astype(jnp.bfloat16)


def cross_attend(query, pool, owner, valid):
    requests, features = query.shape
    heads = features // DH
    pick = (jnp.arange(features)[:, None] // DH == jnp.arange(heads)[None, :])
    spread = jnp.where(pick.T[None], query[:, None, :], 0).reshape(requests * heads, features)
    scores = lax.dot_general(
        spread, pool[0], (((1,), (1,)), ((), ())), preferred_element_type=jnp.float32
    )
    column = jnp.arange(requests * heads) // heads
    mask = (column[:, None] == owner[None, :]) & valid[None, :]
    top = jnp.max(jnp.where(mask, scores, LOWEST), axis=1, keepdims=True)
    weights = jnp.where(mask, jnp.exp(jnp.where(mask, scores, top) - top), 0.0)
    total = jnp.sum(weights, axis=1).reshape(requests, heads)
    mixed = jnp.dot(weights.astype(jnp.bfloat16), pool[1], preferred_element_type=jnp.float32)
    mixed = jnp.sum(
        jnp.where(pick.T[None], mixed.reshape(requests, heads, features), 0.0), axis=1
    )
    top = jnp.repeat(top.reshape(requests, heads), DH, axis=1)
    packed = jnp.concatenate([mixed, top, jnp.repeat(total, DH, axis=1)], axis=1)
    return exchange(packed, features, functools.partial(merged, features), 3).astype(jnp.bfloat16)


def local(
    token_ids,
    slot_of,
    lengths,
    block_table,
    kv_pool,
    self_cache,
    embedding,
    norm_self,
    norm_cross,
    norm_ffn,
    w_self_qkv,
    w_self_out,
    w_cross_q,
    w_cross_out,
    w_in,
    w_out,
):
    dev_count = lax.axis_size("dev")
    requests, max_blocks = block_table.shape
    own = requests // dev_count
    half_inner = w_cross_q.shape[1]
    here = lax.axis_index("dev")
    blocks, rows_here = kv_pool.shape[1:3]
    block_rows = rows_here * dev_count

    slot_hot = slot_of[:, None] == jnp.arange(requests)[None, :]
    ids_slot = jnp.sum(jnp.where(slot_hot, token_ids[0][:, None], 0), axis=0)

    place = slot_of[:, None] * max_blocks + jnp.arange(max_blocks)[None, :] + 1
    hit = block_table.reshape(-1)[:, None] == jnp.arange(blocks)[None, :]
    holder = jnp.sum(jnp.where(hit, place.reshape(-1)[:, None], 0), axis=0) - 1
    span = jnp.sum(jnp.where(hit, jnp.repeat(lengths, max_blocks)[:, None], 0), axis=0)
    first = (holder % max_blocks) * block_rows + here * rows_here
    valid = (first[:, None] + jnp.arange(rows_here)[None, :] < span[:, None]).reshape(-1)
    owner = jnp.repeat(jnp.where(holder >= 0, holder // max_blocks, -1), rows_here)
    pool = kv_pool.reshape(2, blocks * rows_here, half_inner)

    resid = embed(ids_slot, embedding)
    width = resid.shape[1] * dev_count
    summed = functools.partial(scaled_sum, width)
    qkv = project(resid, norm_self, w_self_qkv.reshape(w_self_qkv.shape[0], -1))
    qkv = exchange(qkv, 3 * half_inner, summed, 0, spread=False)
    qkv = qkv.astype(jnp.bfloat16).reshape(own, 3, half_inner)
    mixed = self_attend(qkv[:, 0], qkv[:, 1], qkv[:, 2], self_cache).astype(jnp.float32)
    mixed = exchange(mixed, half_inner, unchanged, 1, scatter=False).astype(jnp.bfloat16)
    resid = resid + output(mixed, w_self_out)

    query = exchange(project(resid, norm_cross, w_cross_q), half_inner, summed, 2)
    mixed = cross_attend(query.astype(jnp.bfloat16), pool, owner, valid)
    resid = resid + output(mixed, w_cross_out)

    gated = project(resid, norm_ffn, w_in.reshape(w_in.shape[0], -1))
    hidden = exchange(gated, w_in.shape[2], functools.partial(gated_sum, width), 4)
    resid = resid + output(hidden.astype(jnp.bfloat16), w_out)
    out = jnp.dot(
        slot_hot.astype(jnp.bfloat16), resid.astype(jnp.bfloat16), preferred_element_type=jnp.float32
    )
    return out.astype(jnp.bfloat16)[None]


def solution(mesh):
    in_specs = (
        P(),
        P(),
        P(),
        P(),
        P(None, None, "dev", "section"),
        P(None, "dev", None, "section"),
        P(None, "dev"),
        P("dev"),
        P("dev"),
        P("dev"),
        P("dev", None, "section"),
        P("section", "dev"),
        P("dev", "section"),
        P("section", "dev"),
        P("dev", None, "section"),
        P("section", "dev"),
    )
    out_specs = P(None, None, "dev")
    return jax.shard_map(local, mesh=mesh, in_specs=in_specs, out_specs=out_specs, check_vma=False)
```

```python
import functools

import jax
import jax.numpy as jnp
from jax import lax
from jax.experimental import pallas as pl
from jax.experimental.pallas import tpu as pltpu
from jax.sharding import PartitionSpec as P

DH = 64
EPS = 1e-06
LANES = 128
LOWEST = -1e30


def exchange_kernel(n, scatter, spread, combine, x_ref, out_ref, *scratch):
    scratch = list(scratch)
    me = lax.axis_index("dev")
    section = lax.axis_index("section")

    def peer(step):
        return (section, lax.rem(me + step, n))

    barrier = pltpu.get_barrier_semaphore()

    @pl.loop(1, n, unroll=n <= 16)
    def _(step):
        pl.semaphore_signal(barrier, inc=1, device_id=peer(step), device_id_type=pl.DeviceIdType.MESH)

    pl.semaphore_wait(barrier, n - 1)

    if scatter:
        held, sent, got = scratch[:3]
        scratch = scratch[3:]

        def chunk(step):
            return pltpu.make_async_remote_copy(
                src_ref=x_ref.at[lax.rem(me + step, n)],
                dst_ref=held.at[step],
                send_sem=sent.at[step],
                recv_sem=got.at[step],
                device_id=peer(step),
                device_id_type=pl.DeviceIdType.MESH,
            )

        @pl.loop(1, n, unroll=n <= 16)
        def _(step):
            chunk(step).start()

        held[0] = x_ref[me]

        @pl.loop(1, n, unroll=n <= 16)
        def _(step):
            chunk(step).wait()

        result = combine(held)
    else:
        result = combine(x_ref)

    if not spread:
        out_ref[...] = result
        return
    mine, full, sent, got = scratch
    mine[...] = result

    def row(step):
        return pltpu.make_async_remote_copy(
            src_ref=mine,
            dst_ref=full.at[me],
            send_sem=sent.at[step],
            recv_sem=got.at[step],
            device_id=peer(step),
            device_id_type=pl.DeviceIdType.MESH,
        )

    @pl.loop(1, n, unroll=n <= 16)
    def _(step):
        row(step).start()

    full[me] = result

    @pl.loop(1, n, unroll=n <= 16)
    def _(step):
        row(step).wait()

    out_ref[...] = full[...]


def exchange(x, columns, combine, collective_id, scatter=True, spread=True):
    n = lax.axis_size("dev")
    own = x.shape[0] // n if scatter else x.shape[0]
    width = x.shape[1]
    scratch = []
    if scatter:
        x = x.reshape(n, own, width)
        scratch += [pltpu.VMEM((n, own, width), jnp.float32)] + [pltpu.SemaphoreType.DMA((n,))] * 2
    if spread:
        scratch += [pltpu.VMEM((own, columns), jnp.float32), pltpu.VMEM((n, own, columns), jnp.float32)]
        scratch += [pltpu.SemaphoreType.DMA((n,))] * 2
    result = pl.pallas_call(
        functools.partial(exchange_kernel, n, scatter, spread, combine),
        out_shape=jax.ShapeDtypeStruct((n, own, columns) if spread else (own, columns), jnp.float32),
        in_specs=[pl.BlockSpec(memory_space=pltpu.VMEM)],
        out_specs=pl.BlockSpec(memory_space=pltpu.VMEM),
        scratch_shapes=scratch,
        compiler_params=pltpu.CompilerParams(
            collective_id=collective_id, has_side_effects=True, vmem_limit_bytes=48 * 1024 * 1024
        ),
    )(x)
    return result.reshape(-1, columns)


def scaled_sum(width, held):
    total = jnp.sum(held[...], axis=0)
    squares = jnp.max(total[:, -LANES:], axis=1, keepdims=True)
    return total[:, :-LANES] * lax.rsqrt(squares / width + EPS)


def gated_sum(width, held):
    gated = scaled_sum(width, held)
    units = gated.shape[1] // 2
    gate = gated[:, :units]
    bent = 0.7978845608028654 * (gate + 0.044715 * (gate * gate * gate))
    return 0.5 * gate * (1.0 + jnp.tanh(bent)) * gated[:, units:]


def merged(features, held):
    parts = held[...]
    mixed, top, total = (parts[:, :, i * features : (i + 1) * features] for i in range(3))
    factor = jnp.exp(top - jnp.max(top, axis=0)[None])
    return jnp.sum(factor * mixed, axis=0) / jnp.sum(factor * total, axis=0)


def unchanged(ref):
    return ref[...]


def project(resid, gain, weight):
    scaled = (resid * gain[None, :]).astype(jnp.bfloat16)
    part = jnp.dot(scaled, weight, preferred_element_type=jnp.float32)
    squares = jnp.sum(resid * resid, axis=1, keepdims=True)
    return jnp.concatenate([part, jnp.broadcast_to(squares, (resid.shape[0], LANES))], axis=1)


def embed_kernel(window, ids_ref, table_ref, out_ref, held, sem):
    requests = out_ref.shape[0]

    def fetch(index):
        first = pl.multiple_of(ids_ref[index] // window * window, window)
        return pltpu.make_async_copy(
            table_ref.at[pl.ds(first, window)], held.at[index], sem.at[index]
        )

    @pl.loop(0, requests)
    def _(index):
        fetch(index).start()

    @pl.loop(0, requests)
    def _(index):
        fetch(index).wait()
        rows = held[index].astype(jnp.float32)
        here = lax.broadcasted_iota(jnp.int32, rows.shape, 0) == ids_ref[index] % window
        out_ref[pl.ds(index, 1)] = jnp.sum(jnp.where(here, rows, 0.0), axis=0, keepdims=True)


def embed(ids, table):
    window = 16
    requests, width = ids.shape[0], table.shape[1]
    if table.shape[0] % window:
        return table[ids].astype(jnp.float32)
    return pl.pallas_call(
        functools.partial(embed_kernel, window),
        out_shape=jax.ShapeDtypeStruct((requests, width), jnp.float32),
        in_specs=[pl.BlockSpec(memory_space=pltpu.SMEM), pl.BlockSpec(memory_space=pl.ANY)],
        out_specs=pl.BlockSpec(memory_space=pltpu.VMEM),
        scratch_shapes=[
            pltpu.VMEM((requests, window, width), table.dtype),
            pltpu.SemaphoreType.DMA((requests,)),
        ],
    )(ids, table)


def output(active, weight):
    return lax.psum(jnp.dot(active, weight, preferred_element_type=jnp.float32), "section")


def self_attend(query, key, value, cache):
    own, features = query.shape
    heads = features // DH
    pick = (jnp.arange(features)[:, None] // DH == jnp.arange(heads)[None, :])
    spread = jnp.where(pick[None], query[:, :, None], 0).astype(jnp.bfloat16)
    scores = jnp.einsum("rjf,rfh->rjh", cache[0], spread, preferred_element_type=jnp.float32)
    fresh = jnp.sum(
        (query.astype(jnp.float32) * key.astype(jnp.float32)).reshape(own, heads, DH), axis=2
    )
    top = jnp.maximum(jnp.max(scores, axis=1), fresh)
    weights = jnp.exp(scores - top[:, None, :])
    weight = jnp.exp(fresh - top)
    total = jnp.sum(weights, axis=1) + weight
    mixed = jnp.einsum(
        "rjh,rjf->rhf", weights.astype(jnp.bfloat16), cache[1], preferred_element_type=jnp.float32
    )
    mixed = jnp.sum(jnp.where(pick.T[None], mixed, 0.0), axis=1)
    wide = jnp.repeat(weight.astype(jnp.bfloat16).astype(jnp.float32), DH, axis=1)
    mixed = mixed + wide * value.astype(jnp.float32)
    return (mixed / jnp.repeat(total, DH, axis=1)).astype(jnp.bfloat16)


def cross_attend(query, pool, owner, valid):
    requests, features = query.shape
    heads = features // DH
    pick = (jnp.arange(features)[:, None] // DH == jnp.arange(heads)[None, :])
    spread = jnp.where(pick.T[None], query[:, None, :], 0).reshape(requests * heads, features)
    scores = lax.dot_general(
        spread, pool[0], (((1,), (1,)), ((), ())), preferred_element_type=jnp.float32
    )
    column = jnp.arange(requests * heads) // heads
    mask = (column[:, None] == owner[None, :]) & valid[None, :]
    top = jnp.max(jnp.where(mask, scores, LOWEST), axis=1, keepdims=True)
    weights = jnp.where(mask, jnp.exp(jnp.where(mask, scores, top) - top), 0.0)
    total = jnp.sum(weights, axis=1).reshape(requests, heads)
    mixed = jnp.dot(weights.astype(jnp.bfloat16), pool[1], preferred_element_type=jnp.float32)
    mixed = jnp.sum(
        jnp.where(pick.T[None], mixed.reshape(requests, heads, features), 0.0), axis=1
    )
    top = jnp.repeat(top.reshape(requests, heads), DH, axis=1)
    packed = jnp.concatenate([mixed, top, jnp.repeat(total, DH, axis=1)], axis=1)
    return exchange(packed, features, functools.partial(merged, features), 3).astype(jnp.bfloat16)


def local(
    token_ids,
    slot_of,
    lengths,
    block_table,
    kv_pool,
    self_cache,
    embedding,
    norm_self,
    norm_cross,
    norm_ffn,
    w_self_qkv,
    w_self_out,
    w_cross_q,
    w_cross_out,
    w_in,
    w_out,
):
    dev_count = lax.axis_size("dev")
    requests, max_blocks = block_table.shape
    own = requests // dev_count
    half_inner = w_cross_q.shape[1]
    here = lax.axis_index("dev")
    blocks, rows_here = kv_pool.shape[1:3]
    block_rows = rows_here * dev_count

    slot_hot = slot_of[:, None] == jnp.arange(requests)[None, :]
    ids_slot = jnp.sum(jnp.where(slot_hot, token_ids[0][:, None], 0), axis=0)

    place = slot_of[:, None] * max_blocks + jnp.arange(max_blocks)[None, :] + 1
    hit = block_table.reshape(-1)[:, None] == jnp.arange(blocks)[None, :]
    holder = jnp.sum(jnp.where(hit, place.reshape(-1)[:, None], 0), axis=0) - 1
    span = jnp.sum(jnp.where(hit, jnp.repeat(lengths, max_blocks)[:, None], 0), axis=0)
    first = (holder % max_blocks) * block_rows + here * rows_here
    valid = (first[:, None] + jnp.arange(rows_here)[None, :] < span[:, None]).reshape(-1)
    owner = jnp.repeat(jnp.where(holder >= 0, holder // max_blocks, -1), rows_here)
    pool = kv_pool.reshape(2, blocks * rows_here, half_inner)

    resid = embed(ids_slot, embedding)
    width = resid.shape[1] * dev_count
    summed = functools.partial(scaled_sum, width)
    qkv = project(resid, norm_self, w_self_qkv.reshape(w_self_qkv.shape[0], -1))
    qkv = exchange(qkv, 3 * half_inner, summed, 0, spread=False)
    qkv = qkv.astype(jnp.bfloat16).reshape(own, 3, half_inner)
    mixed = self_attend(qkv[:, 0], qkv[:, 1], qkv[:, 2], self_cache).astype(jnp.float32)
    mixed = exchange(mixed, half_inner, unchanged, 1, scatter=False).astype(jnp.bfloat16)
    resid = resid + output(mixed, w_self_out)

    query = exchange(project(resid, norm_cross, w_cross_q), half_inner, summed, 2)
    mixed = cross_attend(query.astype(jnp.bfloat16), pool, owner, valid)
    resid = resid + output(mixed, w_cross_out)

    gated = project(resid, norm_ffn, w_in.reshape(w_in.shape[0], -1))
    hidden = exchange(gated, w_in.shape[2], functools.partial(gated_sum, width), 4)
    resid = resid + output(hidden.astype(jnp.bfloat16), w_out)
    out = jnp.dot(
        slot_hot.astype(jnp.bfloat16), resid.astype(jnp.bfloat16), preferred_element_type=jnp.float32
    )
    return out.astype(jnp.bfloat16)[None]


def solution(mesh):
    in_specs = (
        P(),
        P(),
        P(),
        P(),
        P(None, None, "dev", "section"),
        P(None, "dev", None, "section"),
        P(None, "dev"),
        P("dev"),
        P("dev"),
        P("dev"),
        P("dev", None, "section"),
        P("section", "dev"),
        P("dev", "section"),
        P("section", "dev"),
        P("dev", None, "section"),
        P("section", "dev"),
    )
    out_specs = P(None, None, "dev")
    return jax.shard_map(local, mesh=mesh, in_specs=in_specs, out_specs=out_specs, check_vma=False)
```

```python
import functools

import jax
import jax.numpy as jnp
from jax import lax
from jax.experimental import pallas as pl
from jax.experimental.pallas import tpu as pltpu
from jax.sharding import PartitionSpec as P

DH = 64
EPS = 1e-06
LANES = 128
LOWEST = -1e30


def exchange_kernel(n, scatter, spread, combine, x_ref, out_ref, *scratch):
    scratch = list(scratch)
    me = lax.axis_index("dev")
    section = lax.axis_index("section")

    def peer(step):
        return (section, lax.rem(me + step, n))

    barrier = pltpu.get_barrier_semaphore()

    @pl.loop(1, n)
    def _(step):
        pl.semaphore_signal(barrier, inc=1, device_id=peer(step), device_id_type=pl.DeviceIdType.MESH)

    pl.semaphore_wait(barrier, n - 1)

    if scatter:
        held, sent, got = scratch[:3]
        scratch = scratch[3:]

        def chunk(step):
            return pltpu.make_async_remote_copy(
                src_ref=x_ref.at[lax.rem(me + step, n)],
                dst_ref=held.at[step],
                send_sem=sent.at[step],
                recv_sem=got.at[step],
                device_id=peer(step),
                device_id_type=pl.DeviceIdType.MESH,
            )

        @pl.loop(1, n)
        def _(step):
            chunk(step).start()

        held[0] = x_ref[me]

        @pl.loop(1, n)
        def _(step):
            chunk(step).wait()

        result = combine(held)
    else:
        result = combine(x_ref)

    if not spread:
        out_ref[...] = result
        return
    mine, full, sent, got = scratch
    mine[...] = result

    def row(step):
        return pltpu.make_async_remote_copy(
            src_ref=mine,
            dst_ref=full.at[me],
            send_sem=sent.at[step],
            recv_sem=got.at[step],
            device_id=peer(step),
            device_id_type=pl.DeviceIdType.MESH,
        )

    @pl.loop(1, n)
    def _(step):
        row(step).start()

    full[me] = result

    @pl.loop(1, n)
    def _(step):
        row(step).wait()

    out_ref[...] = full[...]


def exchange(x, columns, combine, collective_id, scatter=True, spread=True):
    n = lax.axis_size("dev")
    own = x.shape[0] // n if scatter else x.shape[0]
    width = x.shape[1]
    scratch = []
    if scatter:
        x = x.reshape(n, own, width)
        scratch += [pltpu.VMEM((n, own, width), jnp.float32)] + [pltpu.SemaphoreType.DMA((n,))] * 2
    if spread:
        scratch += [pltpu.VMEM((own, columns), jnp.float32), pltpu.VMEM((n, own, columns), jnp.float32)]
        scratch += [pltpu.SemaphoreType.DMA((n,))] * 2
    result = pl.pallas_call(
        functools.partial(exchange_kernel, n, scatter, spread, combine),
        out_shape=jax.ShapeDtypeStruct((n, own, columns) if spread else (own, columns), jnp.float32),
        in_specs=[pl.BlockSpec(memory_space=pltpu.VMEM)],
        out_specs=pl.BlockSpec(memory_space=pltpu.VMEM),
        scratch_shapes=scratch,
        compiler_params=pltpu.CompilerParams(
            collective_id=collective_id, has_side_effects=True, vmem_limit_bytes=48 * 1024 * 1024
        ),
    )(x)
    return result.reshape(-1, columns)


def scaled_sum(width, held):
    total = jnp.sum(held[...], axis=0)
    squares = jnp.max(total[:, -LANES:], axis=1, keepdims=True)
    return total[:, :-LANES] * lax.rsqrt(squares / width + EPS)


def gated_sum(width, held):
    gated = scaled_sum(width, held)
    units = gated.shape[1] // 2
    gate = gated[:, :units]
    bent = 0.7978845608028654 * (gate + 0.044715 * (gate * gate * gate))
    return 0.5 * gate * (1.0 + jnp.tanh(bent)) * gated[:, units:]


def merged(features, held):
    parts = held[...]
    mixed, top, total = (parts[:, :, i * features : (i + 1) * features] for i in range(3))
    factor = jnp.exp(top - jnp.max(top, axis=0)[None])
    return jnp.sum(factor * mixed, axis=0) / jnp.sum(factor * total, axis=0)


def unchanged(ref):
    return ref[...]


def project(resid, gain, weight):
    scaled = (resid * gain[None, :]).astype(jnp.bfloat16)
    slices = [weight] if weight.ndim == 2 else [weight[:, i] for i in range(weight.shape[1])]
    parts = [jnp.dot(scaled, each, preferred_element_type=jnp.float32) for each in slices]
    squares = jnp.sum(resid * resid, axis=1, keepdims=True)
    return jnp.concatenate([*parts, jnp.broadcast_to(squares, (resid.shape[0], LANES))], axis=1)


def embed_kernel(window, ids_ref, table_ref, out_ref, held, sem):
    requests = out_ref.shape[0]

    def fetch(index):
        first = pl.multiple_of(ids_ref[index] // window * window, window)
        return pltpu.make_async_copy(
            table_ref.at[pl.ds(first, window)], held.at[index], sem.at[index]
        )

    @pl.loop(0, requests)
    def _(index):
        fetch(index).start()

    @pl.loop(0, requests)
    def _(index):
        fetch(index).wait()
        rows = held[index].astype(jnp.float32)
        here = lax.broadcasted_iota(jnp.int32, rows.shape, 0) == ids_ref[index] % window
        out_ref[pl.ds(index, 1)] = jnp.sum(jnp.where(here, rows, 0.0), axis=0, keepdims=True)


def embed(ids, table):
    window = 16
    requests, width = ids.shape[0], table.shape[1]
    if table.shape[0] % window:
        return table[ids].astype(jnp.float32)
    return pl.pallas_call(
        functools.partial(embed_kernel, window),
        out_shape=jax.ShapeDtypeStruct((requests, width), jnp.float32),
        in_specs=[pl.BlockSpec(memory_space=pltpu.SMEM), pl.BlockSpec(memory_space=pl.ANY)],
        out_specs=pl.BlockSpec(memory_space=pltpu.VMEM),
        scratch_shapes=[
            pltpu.VMEM((requests, window, width), table.dtype),
            pltpu.SemaphoreType.DMA((requests,)),
        ],
    )(ids, table)


def output(active, weight):
    return lax.psum(jnp.dot(active, weight, preferred_element_type=jnp.float32), "section")


def self_attend(query, key, value, cache):
    own, features = query.shape
    heads = features // DH
    pick = (jnp.arange(features)[:, None] // DH == jnp.arange(heads)[None, :])
    spread = jnp.where(pick[None], query[:, :, None], 0).astype(jnp.bfloat16)
    scores = jnp.einsum("rjf,rfh->rjh", cache[0], spread, preferred_element_type=jnp.float32)
    fresh = jnp.sum(
        (query.astype(jnp.float32) * key.astype(jnp.float32)).reshape(own, heads, DH), axis=2
    )
    top = jnp.maximum(jnp.max(scores, axis=1), fresh)
    weights = jnp.exp(scores - top[:, None, :])
    weight = jnp.exp(fresh - top)
    total = jnp.sum(weights, axis=1) + weight
    mixed = jnp.einsum(
        "rjh,rjf->rhf", weights.astype(jnp.bfloat16), cache[1], preferred_element_type=jnp.float32
    )
    mixed = jnp.sum(jnp.where(pick.T[None], mixed, 0.0), axis=1)
    wide = jnp.repeat(weight.astype(jnp.bfloat16).astype(jnp.float32), DH, axis=1)
    mixed = mixed + wide * value.astype(jnp.float32)
    return (mixed / jnp.repeat(total, DH, axis=1)).astype(jnp.bfloat16)


def cross_attend(query, pool, owner, valid):
    requests, features = query.shape
    heads = features // DH
    pick = (jnp.arange(features)[:, None] // DH == jnp.arange(heads)[None, :])
    spread = jnp.where(pick.T[None], query[:, None, :], 0).reshape(requests * heads, features)
    scores = lax.dot_general(
        spread, pool[0], (((1,), (1,)), ((), ())), preferred_element_type=jnp.float32
    )
    column = jnp.arange(requests * heads) // heads
    mask = (column[:, None] == owner[None, :]) & valid[None, :]
    top = jnp.max(jnp.where(mask, scores, LOWEST), axis=1, keepdims=True)
    weights = jnp.where(mask, jnp.exp(jnp.where(mask, scores, top) - top), 0.0)
    total = jnp.sum(weights, axis=1).reshape(requests, heads)
    mixed = jnp.dot(weights.astype(jnp.bfloat16), pool[1], preferred_element_type=jnp.float32)
    mixed = jnp.sum(
        jnp.where(pick.T[None], mixed.reshape(requests, heads, features), 0.0), axis=1
    )
    top = jnp.repeat(top.reshape(requests, heads), DH, axis=1)
    packed = jnp.concatenate([mixed, top, jnp.repeat(total, DH, axis=1)], axis=1)
    return exchange(packed, features, functools.partial(merged, features), 3).astype(jnp.bfloat16)


def local(
    token_ids,
    slot_of,
    lengths,
    block_table,
    kv_pool,
    self_cache,
    embedding,
    norm_self,
    norm_cross,
    norm_ffn,
    w_self_qkv,
    w_self_out,
    w_cross_q,
    w_cross_out,
    w_in,
    w_out,
):
    dev_count = lax.axis_size("dev")
    requests, max_blocks = block_table.shape
    own = requests // dev_count
    half_inner = w_cross_q.shape[1]
    here = lax.axis_index("dev")
    blocks, rows_here = kv_pool.shape[1:3]
    block_rows = rows_here * dev_count

    slot_hot = slot_of[:, None] == jnp.arange(requests)[None, :]
    ids_slot = jnp.sum(jnp.where(slot_hot, token_ids[0][:, None], 0), axis=0)

    place = slot_of[:, None] * max_blocks + jnp.arange(max_blocks)[None, :] + 1
    hit = block_table.reshape(-1)[:, None] == jnp.arange(blocks)[None, :]
    holder = jnp.sum(jnp.where(hit, place.reshape(-1)[:, None], 0), axis=0) - 1
    span = jnp.sum(jnp.where(hit, jnp.repeat(lengths, max_blocks)[:, None], 0), axis=0)
    first = (holder % max_blocks) * block_rows + here * rows_here
    valid = (first[:, None] + jnp.arange(rows_here)[None, :] < span[:, None]).reshape(-1)
    owner = jnp.repeat(jnp.where(holder >= 0, holder // max_blocks, -1), rows_here)
    pool = kv_pool.reshape(2, blocks * rows_here, half_inner)

    resid = embed(ids_slot, embedding)
    width = resid.shape[1] * dev_count
    summed = functools.partial(scaled_sum, width)
    qkv = project(resid, norm_self, w_self_qkv)
    qkv = exchange(qkv, 3 * half_inner, summed, 0, spread=False)
    qkv = qkv.astype(jnp.bfloat16).reshape(own, 3, half_inner)
    mixed = self_attend(qkv[:, 0], qkv[:, 1], qkv[:, 2], self_cache).astype(jnp.float32)
    mixed = exchange(mixed, half_inner, unchanged, 1, scatter=False).astype(jnp.bfloat16)
    resid = resid + output(mixed, w_self_out)

    query = exchange(project(resid, norm_cross, w_cross_q), half_inner, summed, 2)
    mixed = cross_attend(query.astype(jnp.bfloat16), pool, owner, valid)
    resid = resid + output(mixed, w_cross_out)

    gated = project(resid, norm_ffn, w_in)
    hidden = exchange(gated, w_in.shape[2], functools.partial(gated_sum, width), 4)
    resid = resid + output(hidden.astype(jnp.bfloat16), w_out)
    out = jnp.dot(
        slot_hot.astype(jnp.bfloat16), resid.astype(jnp.bfloat16), preferred_element_type=jnp.float32
    )
    return out.astype(jnp.bfloat16)[None]


def solution(mesh):
    in_specs = (
        P(),
        P(),
        P(),
        P(),
        P(None, None, "dev", "section"),
        P(None, "dev", None, "section"),
        P(None, "dev"),
        P("dev"),
        P("dev"),
        P("dev"),
        P("dev", None, "section"),
        P("section", "dev"),
        P("dev", "section"),
        P("section", "dev"),
        P("dev", None, "section"),
        P("section", "dev"),
    )
    out_specs = P(None, None, "dev")
    return jax.shard_map(local, mesh=mesh, in_specs=in_specs, out_specs=out_specs, check_vma=False)
```
